32 devices in a mesh: ha: 2 (over y), wa: 16 (over z, x, core).
Axes of the slice: x: 2, y: 2, z: 4, core: 2. Of those that a mesh axis runs over, the one named last changes fastest.
Arguments:
- latent: bfloat16 [16, 1, 3, 16, 128], P('wa', None, None, 'ha'), may hold values from -64 to 64
- conv_in_weight: bfloat16 [3, 3, 3, 16, 512], replicated, may hold values from -0.3125 to 0.3125
- conv_in_bias: float32 [512], replicated, may hold values from -3 to 3
- norm1_gain: float32 [512], replicated, may hold values from 0.5 to 1.5
- norm1_shift: float32 [512], replicated, may hold values from -3 to 3
- conv1_weight: bfloat16 [3, 3, 3, 512, 512], replicated, may hold values from -0.0546875 to 0.0546875
- conv1_bias: float32 [512], replicated, may hold values from -3 to 3
- norm2_gain: float32 [512], replicated, may hold values from 0.5 to 1.5
- norm2_shift: float32 [512], replicated, may hold values from -3 to 3
Outputs:
- decoded: bfloat16 [1, 3, 16, 128, 512], P(None, None, 'ha', 'wa')
The draws below stay inside these ranges and needn't reach their ends.
All inputs are finite; a program needn't handle non-finite values.
Results may differ from the reference program's by a relative error of at most 0.0042.
Values may be sent and summed in bfloat16 or wider, within the bound.
A program may use at most 64 MiB of HBM per device.

```python
import jax
import jax.numpy as jnp
from jax import lax

CHANNELS = 512
LATENT = 16
GROUPS = 32
VIDEOS = 1
FRAMES = 3
HEIGHT = 16
WIDTH = 128


def draw_latent(key, part):
    key = jax.random.fold_in(key, 11)
    streams = jax.random.split(key, 4)
    col_pos = jnp.arange(WIDTH, dtype=jnp.float32) / WIDTH
    row_rough = jnp.exp(jax.random.uniform(streams[0], (HEIGHT,), jnp.float32, -0.7, 0.7))
    col_rough = jnp.exp(jax.random.uniform(streams[1], (WIDTH,), jnp.float32, -0.7, 0.7))
    channel_scale = jnp.exp(jax.random.uniform(streams[2], (LATENT,), jnp.float32, -0.7, 0.7))
    dims = (LATENT, VIDEOS, FRAMES, HEIGHT, WIDTH)
    noise_field = jnp.clip(jax.random.normal(streams[3], dims, jnp.float32), -5.0, 5.0)
    trend = jnp.exp(jnp.log(3.0) * col_pos)[None, :] * jnp.ones((HEIGHT, 1), jnp.float32)
    grid_scale = trend * row_rough[:, None] * col_rough[None, :]
    result = 0.5 * noise_field * grid_scale * channel_scale[:, None, None, None, None]
    return result.astype(jnp.bfloat16)


def normal_values(own_key, shape, width, bound, held_as=jnp.bfloat16):
    array = width * jax.random.normal(own_key, shape, jnp.float32)
    return jnp.clip(array, min=-bound, max=bound).astype(held_as)


def setup_inputs(seed: int = 0) -> dict:
    seeds = jax.random.split(jax.random.key(seed), 10)
    return {
        "latent": draw_latent(jax.random.fold_in(seeds[9], 71), 0),
        "conv_in_weight": normal_values(seeds[1], (3, 3, 3, LATENT, CHANNELS), (27 * LATENT) ** -0.5, 0.3125),
        "conv_in_bias": normal_values(seeds[2], (CHANNELS,), 0.5, 3.0, jnp.float32),
        "norm1_gain": jnp.clip(jax.random.uniform(seeds[3], (CHANNELS,), jnp.float32, 0.5, 1.5), 0.5, 1.5),
        "norm1_shift": normal_values(seeds[4], (CHANNELS,), 0.5, 3.0, jnp.float32),
        "conv1_weight": normal_values(seeds[5], (3, 3, 3, CHANNELS, CHANNELS), (27 * CHANNELS) ** -0.5, 0.0546875),
        "conv1_bias": normal_values(seeds[6], (CHANNELS,), 0.5, 3.0, jnp.float32),
        "norm2_gain": jnp.clip(jax.random.uniform(seeds[7], (CHANNELS,), jnp.float32, 0.5, 1.5), 0.5, 1.5),
        "norm2_shift": normal_values(seeds[8], (CHANNELS,), 0.5, 3.0, jnp.float32),
    }


epsilon = 1e-06

def pad_grid(values):
    first = values[:, :1]
    values = jnp.concatenate([first, first, values], axis=1)
    return jnp.pad(values, ((0, 0), (0, 0), (1, 1), (1, 1), (0, 0)), mode='edge')

def conv_frames(padded, weight):
    padded = padded.astype(jnp.float32)
    weight = weight.astype(jnp.float32)
    frames = padded.shape[1] - 2

    def one_frame(frame):
        window = lax.dynamic_slice_in_dim(padded, frame, 3, 1)
        result = lax.conv_general_dilated(window, weight, (1, 1, 1), 'VALID', dimension_numbers=('NDHWC', 'DHWIO', 'NDHWC'))
        return result[:, 0]
    stacked = lax.map(one_frame, jnp.arange(frames, dtype=jnp.int32))
    return jnp.transpose(stacked, (1, 0, 2, 3, 4))

def group_activate(field, norm_gain, norm_shift):
    batch_size = field.shape[0]
    grouped = field.reshape(batch_size, -1, GROUPS, field.shape[-1] // GROUPS)
    group_mean = lax.optimization_barrier(jnp.mean(grouped, axis=(1, 3), keepdims=True))
    variance = lax.optimization_barrier(jnp.mean(jnp.square(grouped - group_mean), axis=(1, 3), keepdims=True))
    normed = ((grouped - group_mean) * lax.rsqrt(variance + epsilon)).reshape(field.shape)
    return jax.nn.silu(normed * norm_gain + norm_shift)

def reference(latent, conv_in_weight, conv_in_bias, norm1_gain, norm1_shift, conv1_weight, conv1_bias, norm2_gain, norm2_shift):
    retiled = jnp.transpose(latent, (1, 2, 3, 4, 0))
    hidden = conv_frames(pad_grid(retiled), conv_in_weight) + conv_in_bias
    active = group_activate(hidden, norm1_gain, norm1_shift).astype(jnp.bfloat16)
    active = lax.optimization_barrier(active)
    convolved = conv_frames(pad_grid(active), conv1_weight) + conv1_bias
    return group_activate(convolved, norm2_gain, norm2_shift).astype(jnp.bfloat16)
```

```python
import functools

import jax
import jax.numpy as jnp
from jax import lax
from jax.experimental import pallas as pl
from jax.experimental.pallas import tpu as pltpu
from jax.sharding import PartitionSpec as P

GROUPS = 32
EPSILON = 1e-06
MESH = pl.DeviceIdType.MESH
LANES = 128
CELL = 16


def lanes_of(rows):
    return lax.broadcasted_iota(jnp.int32, (rows, LANES), 1)


def group_sum(x):
    lane = lanes_of(x.shape[0])
    for s in (1, 2, 4, 8):
        x = x + jnp.where((lane & s) == 0, pltpu.roll(x, LANES - s, 1), pltpu.roll(x, s, 1))
    return x


def to_rows(x):
    return jnp.concatenate([x[:, k * LANES : (k + 1) * LANES] for k in range(4)], axis=0)


def to_lanes(x):
    return jnp.concatenate([x[k : k + 1] for k in range(4)], axis=1)


def pack_stats(total, spread):
    sub = lanes_of(1) & 15
    row = jnp.zeros((1, LANES), jnp.float32)
    for k in range(4):
        row = jnp.where(sub == k, total[k : k + 1], row)
        row = jnp.where(sub == 4 + k, spread[k : k + 1], row)
    return row


def unpack_stats(mean, inverse):
    sub = lanes_of(1) & 15
    rows = [jnp.where(sub == k, mean, 0.0) for k in range(4)]
    rows += [jnp.where(sub == k, inverse, 0.0) for k in range(4)]
    both = group_sum(jnp.concatenate(rows, axis=0))
    return to_lanes(both[:4]), to_lanes(both[4:])


def wait_bytes(ref, sem):
    pltpu.make_async_copy(ref, ref, sem).wait()


def kernel(
    ha,
    wa,
    lat_hbm,
    win_hbm,
    bin_hbm,
    g1_hbm,
    s1_hbm,
    w1_hbm,
    b1_hbm,
    g2_hbm,
    s2_hbm,
    out_ref,
    lat,
    win,
    vec,
    w1,
    pack,
    grid,
    hid,
    cols,
    conv,
    st_send,
    st_recv,
    local_sem,
    win_sem,
    w1_sem,
    lat_send,
    lat_recv,
    stat_send,
    stat_recv,
):
    h, w = lax.axis_index("ha"), lax.axis_index("wa")
    peers = ha * wa - 1

    def peer_of(dh, dw):
        ph, pw = h + dh, w + dw
        return (jnp.where(ph >= ha, ph - ha, ph), jnp.where(pw >= wa, pw - wa, pw))

    @pl.when(h == 0)
    def _():
        grid[0] = jnp.zeros((wa, 3, LANES), jnp.float32)

    @pl.when(h == ha - 1)
    def _():
        grid[2] = jnp.zeros((wa, 3, LANES), jnp.float32)

    lat_copy = pltpu.make_async_copy(lat_hbm, lat, local_sem.at[0])
    lat_copy.start()
    barrier = pltpu.get_barrier_semaphore()
    for dh in range(ha):
        for dw in range(wa):
            if dh or dw:
                pl.semaphore_signal(barrier, inc=1, device_id=peer_of(dh, dw), device_id_type=MESH)
    win_copies = []
    for kt in range(3):
        copy = pltpu.make_async_copy(win_hbm.at[kt], win.at[kt, pl.ds(0, 144)], win_sem.at[kt])
        copy.start()
        win_copies.append(copy)
    vec_copies = []
    for n, source in enumerate((bin_hbm, g1_hbm, s1_hbm, b1_hbm, g2_hbm, s2_hbm)):
        copy = pltpu.make_async_copy(source, vec.at[n], local_sem.at[2 + n])
        copy.start()
        vec_copies.append(copy)
    w1_copies = []
    for kt in range(3):
        copy = pltpu.make_async_copy(w1_hbm.at[kt], w1.at[kt], w1_sem.at[kt])
        copy.start()
        w1_copies.append(copy)

    win[:, 144:, :] = jnp.zeros((3, 112, 512), jnp.bfloat16)

    lat_copy.wait()
    tile = LANES // wa
    lane8 = lanes_of(8)
    row8 = lax.broadcasted_iota(jnp.int32, (8, LANES), 0)
    frames = []
    for t in range(3):
        x = lat[t].astype(jnp.float32)
        frames.append(pltpu.roll(x, 2, 1, stride=CELL, stride_axis=0))
    for dst in range(wa):
        for t in range(3):
            x = pltpu.roll(frames[t], (LANES - tile * dst) % LANES, 1) if dst else frames[t]
            x = jnp.where(lane8 // CELL == row8, x, 0.0)
            pack[dst, t : t + 1, :] = jnp.sum(x, axis=0, keepdims=True)

    pl.semaphore_wait(barrier, peers)

    def send_latent(dh, dw):
        pw = w + dw
        pw = jnp.where(pw >= wa, pw - wa, pw)
        pltpu.make_async_remote_copy(
            src_ref=pack.at[pw],
            dst_ref=grid.at[1 - dh, w],
            send_sem=lat_send.at[1 - dh],
            recv_sem=lat_recv.at[1 - dh],
            device_id=(h + dh, pw),
            device_id_type=MESH,
        ).start()

    pltpu.make_async_copy(pack.at[w], grid.at[1, w], lat_recv.at[1]).start()
    for dw in range(1, wa):
        send_latent(0, dw)

    @pl.when(h > 0)
    def _():
        for dw in range(wa):
            send_latent(-1, dw)

    @pl.when(h < ha - 1)
    def _():
        for dw in range(wa):
            send_latent(1, dw)

    wait_bytes(grid.at[1], lat_recv.at[1])

    @pl.when(h > 0)
    def _():
        wait_bytes(grid.at[0], lat_recv.at[0])

    @pl.when(h < ha - 1)
    def _():
        wait_bytes(grid.at[2], lat_recv.at[2])

    top, bottom = h == 0, h == ha - 1
    left_lane = jnp.where(w == 0, 1, -1)
    right_lane = jnp.where(w == wa - 1, tile + 2, -1)
    lane = lanes_of(wa)
    patches = []
    for t in range(3):
        up, own, down = (grid[s, :, t, :] for s in range(3))
        up = jnp.where(top, pltpu.roll(own, 16, 1), pltpu.roll(up, 32, 1))
        down = jnp.where(bottom, pltpu.roll(own, 48, 1), pltpu.roll(down, 32, 1))
        own = pltpu.roll(own, 32, 1)
        strips = [jnp.where(lane < 32, up, own), jnp.where(lane < 32, own, down)]
        for n in range(2):
            x = strips[n]
            x = jnp.where((lane & 15) == left_lane, pltpu.roll(x, LANES - 1, 1), x)
            strips[n] = jnp.where((lane & 15) == right_lane, pltpu.roll(x, 1, 1), x)
        first, second = strips
        pieces = []
        for ki in range(3):
            for kj in range(3):
                s = ki * CELL + kj
                if s:
                    a, b = pltpu.roll(first, LANES - s, 1), pltpu.roll(second, LANES - s, 1)
                    a = jnp.where(lane < LANES - s, a, b)
                else:
                    a, b = first, second
                pieces.append((a, b))
        pieces.append((jnp.zeros((112, LANES), jnp.float32),) * 2)
        a = jnp.concatenate([p[0] for p in pieces], axis=0).T
        b = jnp.concatenate([p[1] for p in pieces], axis=0).T
        patches.append(jnp.concatenate([a, b[:32]], axis=0).astype(jnp.bfloat16))

    for copy in win_copies + vec_copies:
        copy.wait()

    def product(t, kt):
        return jnp.dot(patches[t], win[kt], preferred_element_type=jnp.float32)

    d00 = product(0, 0) + vec[0]
    d01 = d00 + product(0, 1)
    hid[0] = d01 + product(0, 2)
    hid[1] = d01 + product(1, 2)
    hid[2] = d00 + product(1, 1) + product(2, 2)

    group_cells = 3 * 64 * 16
    all_cells = group_cells * ha * wa
    position = lax.broadcasted_iota(jnp.int32, (160, LANES), 0)
    cell_i, cell_j = position // CELL, position & 15
    inside = (cell_i >= 1) & (cell_i <= 8) & (cell_j >= 1) & (cell_j <= 8)

    def exchange(phase, total, spread):
        mine = pack_stats(total, spread)
        st_send[phase] = mine
        for dh in range(ha):
            for dw in range(wa):
                if dh or dw:
                    pltpu.make_async_remote_copy(
                        src_ref=st_send.at[phase],
                        dst_ref=st_recv.at[phase, dh * wa + dw - 1],
                        send_sem=stat_send.at[phase],
                        recv_sem=stat_recv.at[phase],
                        device_id=peer_of(dh, dw),
                        device_id_type=MESH,
                    ).start()
        wait_bytes(st_recv.at[phase], stat_recv.at[phase])
        theirs = st_recv[phase]
        totals = jnp.sum(theirs, axis=0) + mine
        mean = totals / all_cells
        off = theirs * (1.0 / group_cells) - mean[None]
        off_mine = mine * (1.0 / group_cells) - mean
        between = jnp.sum(off * off, axis=0) + off_mine * off_mine
        spread_all = pltpu.roll(totals, LANES - 4, 1) + between * group_cells
        return unpack_stats(mean, lax.rsqrt(spread_all / all_cells + EPSILON))

    def statistics(blocks):
        sums = []
        for k in range(4):
            sums.append(sum(jnp.sum(b, axis=0, keepdims=True) for b in blocks(k)))
        total = group_sum(jnp.concatenate(sums, axis=0))
        mean = total / group_cells
        spreads = []
        for k in range(4):
            spreads.append(
                sum(jnp.sum(b, axis=0, keepdims=True) for b in blocks(k, mean[k : k + 1]))
            )
        return total, group_sum(jnp.concatenate(spreads, axis=0))

    def hidden_blocks(k, mean=None):
        for t in range(3):
            x = hid[t, :, k * LANES : (k + 1) * LANES]
            if mean is not None:
                x = (x - mean) * (x - mean)
            yield jnp.where(inside, x, 0.0)

    mean, inverse = exchange(0, *statistics(hidden_blocks))
    scale = inverse * vec[1]
    shift = vec[2]

    for copy in w1_copies:
        copy.wait()
    left_row = jnp.where(w == 0, 0, -1)
    right_row = jnp.where(w == wa - 1, 7, -1)
    row = lax.broadcasted_iota(jnp.int32, (10, 8, LANES), 1)
    for t in range(3):
        for k in range(4):
            part = slice(k * LANES, (k + 1) * LANES)
            x = hid[t, :, part]
            x = (x - mean[:, part]) * scale[:, part] + shift[:, part]
            x = (0.5 * x * (1.0 + jnp.tanh(0.5 * x))).reshape(10, 16, LANES)
            middle = x[:, 1:9]
            shifted = [
                jnp.where(row == left_row, middle, x[:, 0:8]),
                middle,
                jnp.where(row == right_row, middle, x[:, 2:10]),
            ]
            for kj in range(3):
                y = shifted[kj]
                y = jnp.concatenate(
                    [
                        jnp.where(top, y[1:2], y[0:1]),
                        y[1:9],
                        jnp.where(bottom, y[8:9], y[9:10]),
                    ],
                    axis=0,
                )
                for ki in range(3):
                    at = (ki * 3 + kj) * 512 + k * LANES
                    cols[t * 64 : (t + 1) * 64, at : at + LANES] = (
                        y[ki : ki + 8].reshape(64, LANES).astype(jnp.bfloat16)
                    )

    def conv_part(kt):
        total = 0.0
        for n in range(9):
            at = slice(n * 512, (n + 1) * 512)
            total += jnp.dot(cols[: 64 * (kt + 1), at], w1[kt, at], preferred_element_type=jnp.float32)
        return total

    c0 = conv_part(0) + vec[3]
    c1 = conv_part(1)
    c01 = c0 + c1[:64]
    c2 = conv_part(2)
    conv[0:64] = c01 + c2[:64]
    conv[64:128] = c01 + c2[64:128]
    conv[128:192] = c0 + c1[64:] + c2[128:]

    def conv_blocks(k, mean=None):
        x = conv[:, k * LANES : (k + 1) * LANES]
        if mean is not None:
            x = (x - mean) * (x - mean)
        yield x

    mean, inverse = exchange(1, *statistics(conv_blocks))
    scale = inverse * vec[4]
    shift = vec[5]
    for k in range(4):
        part = slice(k * LANES, (k + 1) * LANES)
        x = (conv[:, part] - mean[:, part]) * scale[:, part] + shift[:, part]
        out_ref[:, part] = (0.5 * x * (1.0 + jnp.tanh(0.5 * x))).astype(out_ref.dtype)

    wait_bytes(pack.at[pl.ds(0, wa - 1)], lat_send.at[1])

    @pl.when(h > 0)
    def _():
        wait_bytes(pack, lat_send.at[2])

    @pl.when(h < ha - 1)
    def _():
        wait_bytes(pack, lat_send.at[0])

    for phase in range(2):
        wait_bytes(st_recv.at[phase], stat_send.at[phase])


def on_device(ha, wa, latent, w_in, b_in, g1, s1, w1, b1, g2, s2):
    peers = ha * wa - 1
    vectors = [v.reshape(1, 512) for v in (b_in, g1, s1, b1, g2, s2)]
    out = pl.pallas_call(
        functools.partial(kernel, ha, wa),
        out_shape=jax.ShapeDtypeStruct((192, 512), jnp.bfloat16),
        in_specs=[pl.BlockSpec(memory_space=pl.ANY)] * 9,
        out_specs=pl.BlockSpec(memory_space=pltpu.VMEM),
        scratch_shapes=[
            pltpu.VMEM((3, 8, LANES), jnp.bfloat16),
            pltpu.VMEM((3, 256, 512), jnp.bfloat16),
            pltpu.VMEM((6, 1, 512), jnp.float32),
            pltpu.VMEM((3, 4608, 512), jnp.bfloat16),
            pltpu.VMEM((wa, 3, LANES), jnp.float32),
            pltpu.VMEM((3, wa, 3, LANES), jnp.float32),
            pltpu.VMEM((3, 160, 512), jnp.float32),
            pltpu.VMEM((192, 4608), jnp.bfloat16),
            pltpu.VMEM((192, 512), jnp.float32),
            pltpu.VMEM((2, 1, LANES), jnp.float32),
            pltpu.VMEM((2, peers, 1, LANES), jnp.float32),
            pltpu.SemaphoreType.DMA((8,)),
            pltpu.SemaphoreType.DMA((3,)),
            pltpu.SemaphoreType.DMA((3,)),
            pltpu.SemaphoreType.DMA((3,)),
            pltpu.SemaphoreType.DMA((3,)),
            pltpu.SemaphoreType.DMA((2,)),
            pltpu.SemaphoreType.DMA((2,)),
        ],
        compiler_params=pltpu.CompilerParams(
            collective_id=0, has_side_effects=True, vmem_limit_bytes=56 * 1024 * 1024
        ),
    )(
        latent.reshape(3, 8, LANES),
        w_in.reshape(3, 144, 512),
        vectors[0],
        vectors[1],
        vectors[2],
        w1.reshape(3, 4608, 512),
        vectors[3],
        vectors[4],
        vectors[5],
    )
    return out.reshape(1, 3, 8, 8, 512)


def solution(mesh):
    return jax.shard_map(
        functools.partial(on_device, mesh.shape["ha"], mesh.shape["wa"]),
        mesh=mesh,
        in_specs=(P("wa", None, None, "ha", None), P(), P(), P(), P(), P(), P(), P(), P()),
        out_specs=P(None, None, "ha", "wa", None),
        check_vma=False,
    )
```

```python
import functools

import jax
import jax.numpy as jnp
from jax import lax
from jax.experimental import pallas as pl
from jax.experimental.pallas import tpu as pltpu
from jax.sharding import PartitionSpec as P

GROUPS = 32
EPSILON = 1e-06
MESH = pl.DeviceIdType.MESH
LANES = 128
CELL = 16


def lanes_of(rows):
    return lax.broadcasted_iota(jnp.int32, (rows, LANES), 1)


def group_sum(x):
    lane = lanes_of(x.shape[0])
    for s in (1, 2, 4, 8):
        x = x + jnp.where((lane & s) == 0, pltpu.roll(x, LANES - s, 1), pltpu.roll(x, s, 1))
    return x


def to_rows(x):
    return jnp.concatenate([x[:, k * LANES : (k + 1) * LANES] for k in range(4)], axis=0)


def to_lanes(x):
    return jnp.concatenate([x[k : k + 1] for k in range(4)], axis=1)


def pack_stats(total, spread):
    sub = lanes_of(1) & 15
    row = jnp.zeros((1, LANES), jnp.float32)
    for k in range(4):
        row = jnp.where(sub == k, total[k : k + 1], row)
        row = jnp.where(sub == 4 + k, spread[k : k + 1], row)
    return row


def unpack_stats(mean, inverse):
    sub = lanes_of(1) & 15
    rows = [jnp.where(sub == k, mean, 0.0) for k in range(4)]
    rows += [jnp.where(sub == k, inverse, 0.0) for k in range(4)]
    both = group_sum(jnp.concatenate(rows, axis=0))
    return to_lanes(both[:4]), to_lanes(both[4:])


def wait_bytes(ref, sem):
    pltpu.make_async_copy(ref, ref, sem).wait()


def kernel(
    ha,
    wa,
    lat_hbm,
    win_hbm,
    bin_hbm,
    g1_hbm,
    s1_hbm,
    w1_hbm,
    b1_hbm,
    g2_hbm,
    s2_hbm,
    out_ref,
    lat,
    win,
    vec,
    w1,
    pack,
    grid,
    hid,
    cols,
    conv,
    st_send,
    st_recv,
    local_sem,
    win_sem,
    w1_sem,
    lat_send,
    lat_recv,
    stat_send,
    stat_recv,
):
    h, w = lax.axis_index("ha"), lax.axis_index("wa")
    peers = ha * wa - 1

    def peer_of(dh, dw):
        ph, pw = h + dh, w + dw
        return (jnp.where(ph >= ha, ph - ha, ph), jnp.where(pw >= wa, pw - wa, pw))

    @pl.when(h == 0)
    def _():
        grid[0] = jnp.zeros((wa, 3, LANES), jnp.float32)

    @pl.when(h == ha - 1)
    def _():
        grid[2] = jnp.zeros((wa, 3, LANES), jnp.float32)

    lat_copy = pltpu.make_async_copy(lat_hbm, lat, local_sem.at[0])
    lat_copy.start()
    barrier = pltpu.get_barrier_semaphore()
    for dh in range(ha):
        for dw in range(wa):
            if dh or dw:
                pl.semaphore_signal(barrier, inc=1, device_id=peer_of(dh, dw), device_id_type=MESH)
    win_copies = []
    for kt in range(3):
        copy = pltpu.make_async_copy(win_hbm.at[kt], win.at[kt, pl.ds(0, 144)], win_sem.at[kt])
        copy.start()
        win_copies.append(copy)
    vec_copies = []
    for n, source in enumerate((bin_hbm, g1_hbm, s1_hbm, b1_hbm, g2_hbm, s2_hbm)):
        copy = pltpu.make_async_copy(source, vec.at[n], local_sem.at[2 + n])
        copy.start()
        vec_copies.append(copy)
    w1_copies = []
    for kt in range(3):
        copy = pltpu.make_async_copy(w1_hbm.at[kt], w1.at[kt], w1_sem.at[kt])
        copy.start()
        w1_copies.append(copy)

    win[:, 144:, :] = jnp.zeros((3, 112, 512), jnp.bfloat16)

    lat_copy.wait()
    tile = LANES // wa
    lane8 = lanes_of(8)
    row8 = lax.broadcasted_iota(jnp.int32, (8, LANES), 0)
    frames = []
    for t in range(3):
        x = lat[t].astype(jnp.float32)
        frames.append(pltpu.roll(x, 2, 1, stride=CELL, stride_axis=0))
    for dst in range(wa):
        for t in range(3):
            x = pltpu.roll(frames[t], (LANES - tile * dst) % LANES, 1) if dst else frames[t]
            x = jnp.where(lane8 // CELL == row8, x, 0.0)
            pack[dst, t : t + 1, :] = jnp.sum(x, axis=0, keepdims=True)

    pl.semaphore_wait(barrier, peers)

    def send_latent(dh, dw):
        pw = w + dw
        pw = jnp.where(pw >= wa, pw - wa, pw)
        pltpu.make_async_remote_copy(
            src_ref=pack.at[pw],
            dst_ref=grid.at[1 - dh, w],
            send_sem=lat_send.at[1 - dh],
            recv_sem=lat_recv.at[1 - dh],
            device_id=(h + dh, pw),
            device_id_type=MESH,
        ).start()

    pltpu.make_async_copy(pack.at[w], grid.at[1, w], lat_recv.at[1]).start()
    for dw in range(1, wa):
        send_latent(0, dw)

    @pl.when(h > 0)
    def _():
        for dw in range(wa):
            send_latent(-1, dw)

    @pl.when(h < ha - 1)
    def _():
        for dw in range(wa):
            send_latent(1, dw)

    wait_bytes(grid.at[1], lat_recv.at[1])

    @pl.when(h > 0)
    def _():
        wait_bytes(grid.at[0], lat_recv.at[0])

    @pl.when(h < ha - 1)
    def _():
        wait_bytes(grid.at[2], lat_recv.at[2])

    top, bottom = h == 0, h == ha - 1
    left_lane = jnp.where(w == 0, 1, -1)
    right_lane = jnp.where(w == wa - 1, tile + 2, -1)
    lane = lanes_of(wa)
    patches = []
    for t in range(3):
        up, own, down = (grid[s, :, t, :] for s in range(3))
        up = jnp.where(top, pltpu.roll(own, 16, 1), pltpu.roll(up, 32, 1))
        down = jnp.where(bottom, pltpu.roll(own, 48, 1), pltpu.roll(down, 32, 1))
        own = pltpu.roll(own, 32, 1)
        strips = [jnp.where(lane < 32, up, own), jnp.where(lane < 32, own, down)]
        for n in range(2):
            x = strips[n]
            x = jnp.where((lane & 15) == left_lane, pltpu.roll(x, LANES - 1, 1), x)
            strips[n] = jnp.where((lane & 15) == right_lane, pltpu.roll(x, 1, 1), x)
        first, second = strips
        pieces = []
        for ki in range(3):
            for kj in range(3):
                s = ki * CELL + kj
                if s:
                    a, b = pltpu.roll(first, LANES - s, 1), pltpu.roll(second, LANES - s, 1)
                    a = jnp.where(lane < LANES - s, a, b)
                else:
                    a, b = first, second
                pieces.append((a, b))
        pieces.append((jnp.zeros((112, LANES), jnp.float32),) * 2)
        a = jnp.concatenate([p[0] for p in pieces], axis=0).T
        b = jnp.concatenate([p[1] for p in pieces], axis=0).T
        patches.append(jnp.concatenate([a, b[:32]], axis=0).astype(jnp.bfloat16))

    for copy in win_copies + vec_copies:
        copy.wait()

    def product(t, kt):
        return jnp.dot(patches[t], win[kt], preferred_element_type=jnp.float32)

    d00 = product(0, 0) + vec[0]
    d01 = d00 + product(0, 1)
    hid[0] = d01 + product(0, 2)
    hid[1] = d01 + product(1, 2)
    hid[2] = d00 + product(1, 1) + product(2, 2)

    group_cells = 3 * 64 * 16
    all_cells = group_cells * ha * wa
    position = lax.broadcasted_iota(jnp.int32, (160, LANES), 0)
    cell_i, cell_j = position // CELL, position & 15
    inside = (cell_i >= 1) & (cell_i <= 8) & (cell_j >= 1) & (cell_j <= 8)

    def exchange(phase, total, spread):
        mine = pack_stats(total, spread)
        st_send[phase] = mine
        for dh in range(ha):
            for dw in range(wa):
                if dh or dw:
                    pltpu.make_async_remote_copy(
                        src_ref=st_send.at[phase],
                        dst_ref=st_recv.at[phase, dh * wa + dw - 1],
                        send_sem=stat_send.at[phase],
                        recv_sem=stat_recv.at[phase],
                        device_id=peer_of(dh, dw),
                        device_id_type=MESH,
                    ).start()
        wait_bytes(st_recv.at[phase], stat_recv.at[phase])
        theirs = st_recv[phase]
        totals = jnp.sum(theirs, axis=0) + mine
        mean = totals / all_cells
        off = theirs * (1.0 / group_cells) - mean[None]
        off_mine = mine * (1.0 / group_cells) - mean
        between = jnp.sum(off * off, axis=0) + off_mine * off_mine
        spread_all = pltpu.roll(totals, LANES - 4, 1) + between * group_cells
        return unpack_stats(mean, lax.rsqrt(spread_all / all_cells + EPSILON))

    def statistics(blocks):
        sums = []
        for k in range(4):
            sums.append(sum(jnp.sum(b, axis=0, keepdims=True) for b in blocks(k)))
        total = group_sum(jnp.concatenate(sums, axis=0))
        mean = total / group_cells
        spreads = []
        for k in range(4):
            spreads.append(
                sum(jnp.sum(b, axis=0, keepdims=True) for b in blocks(k, mean[k : k + 1]))
            )
        return total, group_sum(jnp.concatenate(spreads, axis=0))

    def hidden_blocks(k, mean=None):
        for t in range(3):
            x = hid[t, :, k * LANES : (k + 1) * LANES]
            if mean is not None:
                x = (x - mean) * (x - mean)
            yield jnp.where(inside, x, 0.0)

    mean, inverse = exchange(0, *statistics(hidden_blocks))
    scale = inverse * vec[1]
    shift = vec[2]

    for copy in w1_copies:
        copy.wait()
    left_row = jnp.where(w == 0, 0, -1)
    right_row = jnp.where(w == wa - 1, 7, -1)
    row = lax.broadcasted_iota(jnp.int32, (10, 8, LANES), 1)
    for t in range(3):
        for k in range(4):
            part = slice(k * LANES, (k + 1) * LANES)
            x = hid[t, :, part]
            x = (x - mean[:, part]) * scale[:, part] + shift[:, part]
            x = (0.5 * x * (1.0 + jnp.tanh(0.5 * x))).reshape(10, 16, LANES)
            middle = x[:, 1:9]
            shifted = [
                jnp.where(row == left_row, middle, x[:, 0:8]),
                middle,
                jnp.where(row == right_row, middle, x[:, 2:10]),
            ]
            for kj in range(3):
                y = shifted[kj]
                y = jnp.concatenate(
                    [
                        jnp.where(top, y[1:2], y[0:1]),
                        y[1:9],
                        jnp.where(bottom, y[8:9], y[9:10]),
                    ],
                    axis=0,
                )
                for ki in range(3):
                    at = (ki * 3 + kj) * 512 + k * LANES
                    cols[t * 64 : (t + 1) * 64, at : at + LANES] = (
                        y[ki : ki + 8].reshape(64, LANES).astype(jnp.bfloat16)
                    )

    def conv_part(kt, part):
        total = 0.0
        for n in range(9):
            at = slice(n * 512, (n + 1) * 512)
            total += jnp.dot(
                cols[: 64 * (kt + 1), at], w1[kt, at, part], preferred_element_type=jnp.float32
            )
        return total

    for n in range(2):
        part = slice(n * 256, (n + 1) * 256)
        c0 = conv_part(0, part) + vec[3, :, part]
        c1 = conv_part(1, part)
        c01 = c0 + c1[:64]
        c2 = conv_part(2, part)
        conv[0:64, part] = c01 + c2[:64]
        conv[64:128, part] = c01 + c2[64:128]
        conv[128:192, part] = c0 + c1[64:] + c2[128:]

    def conv_blocks(k, mean=None):
        x = conv[:, k * LANES : (k + 1) * LANES]
        if mean is not None:
            x = (x - mean) * (x - mean)
        yield x

    mean, inverse = exchange(1, *statistics(conv_blocks))
    scale = inverse * vec[4]
    shift = vec[5]
    for k in range(4):
        part = slice(k * LANES, (k + 1) * LANES)
        x = (conv[:, part] - mean[:, part]) * scale[:, part] + shift[:, part]
        out_ref[:, part] = (0.5 * x * (1.0 + jnp.tanh(0.5 * x))).astype(out_ref.dtype)

    wait_bytes(pack.at[pl.ds(0, wa - 1)], lat_send.at[1])

    @pl.when(h > 0)
    def _():
        wait_bytes(pack, lat_send.at[2])

    @pl.when(h < ha - 1)
    def _():
        wait_bytes(pack, lat_send.at[0])

    for phase in range(2):
        wait_bytes(st_recv.at[phase], stat_send.at[phase])


def on_device(ha, wa, latent, w_in, b_in, g1, s1, w1, b1, g2, s2):
    peers = ha * wa - 1
    vectors = [v.reshape(1, 512) for v in (b_in, g1, s1, b1, g2, s2)]
    out = pl.pallas_call(
        functools.partial(kernel, ha, wa),
        out_shape=jax.ShapeDtypeStruct((192, 512), jnp.bfloat16),
        in_specs=[pl.BlockSpec(memory_space=pl.ANY)] * 9,
        out_specs=pl.BlockSpec(memory_space=pltpu.VMEM),
        scratch_shapes=[
            pltpu.VMEM((3, 8, LANES), jnp.bfloat16),
            pltpu.VMEM((3, 256, 512), jnp.bfloat16),
            pltpu.VMEM((6, 1, 512), jnp.float32),
            pltpu.VMEM((3, 4608, 512), jnp.bfloat16),
            pltpu.VMEM((wa, 3, LANES), jnp.float32),
            pltpu.VMEM((3, wa, 3, LANES), jnp.float32),
            pltpu.VMEM((3, 160, 512), jnp.float32),
            pltpu.VMEM((192, 4608), jnp.bfloat16),
            pltpu.VMEM((192, 512), jnp.float32),
            pltpu.VMEM((2, 1, LANES), jnp.float32),
            pltpu.VMEM((2, peers, 1, LANES), jnp.float32),
            pltpu.SemaphoreType.DMA((8,)),
            pltpu.SemaphoreType.DMA((3,)),
            pltpu.SemaphoreType.DMA((3,)),
            pltpu.SemaphoreType.DMA((3,)),
            pltpu.SemaphoreType.DMA((3,)),
            pltpu.SemaphoreType.DMA((2,)),
            pltpu.SemaphoreType.DMA((2,)),
        ],
        compiler_params=pltpu.CompilerParams(
            collective_id=0, has_side_effects=True, vmem_limit_bytes=56 * 1024 * 1024
        ),
    )(
        latent.reshape(3, 8, LANES),
        w_in.reshape(3, 144, 512),
        vectors[0],
        vectors[1],
        vectors[2],
        w1.reshape(3, 4608, 512),
        vectors[3],
        vectors[4],
        vectors[5],
    )
    return out.reshape(1, 3, 8, 8, 512)


def solution(mesh):
    return jax.shard_map(
        functools.partial(on_device, mesh.shape["ha"], mesh.shape["wa"]),
        mesh=mesh,
        in_specs=(P("wa", None, None, "ha", None), P(), P(), P(), P(), P(), P(), P(), P()),
        out_specs=P(None, None, "ha", "wa", None),
        check_vma=False,
    )
```
